32 devices in a mesh: group: 2 (over x), node: 16 (over z, y, core).
Axes of the slice: x: 2, y: 2, z: 4, core: 2. Of those that a mesh axis runs over, the one named last changes fastest.
Arguments:
- right_side: float32 [120, 12288], P(None, ('group', 'node')), parts along dimension 1, may hold values from -130 to 130
- initial: float32 [120, 12288], P(None, ('group', 'node')), parts along dimension 1, may hold values from -3 to 3
- galerkin_mats: float32 [10, 120, 120], replicated, may hold values from -0.1 to 2.5, as said below
- stiffness_tiles: float32 [10, 96, 4, 128, 128], P(None, ('group', 'node')), parts along dimension 1, may hold values from -0.004 to 0.235, as said below
- block_cols: int32 [96, 4], P(('group', 'node')), parts along dimension 0, may hold values from 0 to 47, as said below
Outputs:
- solution_field: float32 [120, 12288], P(None, ('group', 'node')), parts along dimension 1
- residual: float32 [120, 12288], P(None, ('group', 'node')), parts along dimension 1
The draws below stay inside these ranges and needn't reach their ends.
There are 2 independent parts, one for each index of `group`. The reference program is written for one: setup_inputs(seed, part) draws one part's arguments, and reference() takes and returns one part's arrays. A program takes and returns all parts, laid end to end along the dimension named above; an argument that names none is the same for every part. Nothing has to cross between parts.
Inputs may be any that keep to these rules, and one draw needn't show every extreme that they name: `galerkin_mats`: each G_k is symmetric. `stiffness_tiles`: each K_k is symmetric: the tile of block row b at block column c is the transpose of the tile of row c at column b; where b has no block b-1 or b+1, that slot names b and holds zeros. `block_cols`: block row b names b, b-1 and b+1 where they exist (else b again), and one partner block at distance 2 or 3 inside its aligned group of 6 blocks, the partner of that block being b; the order of the slots is arbitrary for each row.
All inputs are finite; a program needn't handle non-finite values.
Results may differ from the reference program's by a relative error of at most 0.0003.
Values sent between devices are 32-bit elements; how exact they have to be, the bound alone decides.
A program may use at most 64 MiB of HBM per device.

```python
import math
import jax
import jax.numpy as jnp
from jax import lax

P_SIZE = 120
KL = 10
BLK = 128
SLOTS = 4
ITERS = 2
NBLK = 48
NODES = 6144


def block_pattern(key):
    base_key = jax.random.fold_in(key, 7)
    group_plan = jax.random.randint(base_key, (NBLK // 6,), 0, 2)
    plan_one = jnp.array([3, 3, 3, -3, -3, -3], jnp.int32)
    plan_two = jnp.array([2, 3, -2, 2, -3, -2], jnp.int32)
    partner = jnp.where(group_plan[:, None] == 0, plan_one[None, :], plan_two[None, :]).reshape(NBLK)
    row_index = jnp.arange(NBLK, dtype=jnp.int32)
    has_left = row_index > 0
    has_right = row_index < NBLK - 1
    columns = jnp.stack([row_index, jnp.where(has_left, row_index - 1, row_index), jnp.where(has_right, row_index + 1, row_index), row_index + partner], axis=1)
    order_keys = jax.random.split(jax.random.fold_in(key, 11), NBLK)
    slot_order = jax.vmap(lambda row_key: jax.random.permutation(row_key, SLOTS))(order_keys)
    return (columns, partner, has_left, has_right, slot_order, row_index)


def draw_block_cols(key, part):
    columns, partner, has_left, has_right, slot_order, row_index = block_pattern(key)
    return columns[row_index[:, None], slot_order].astype(jnp.int32)


def draw_stiffness_tiles(key, part):
    columns, partner, has_left, has_right, slot_order, row_index = block_pattern(key)
    key_diag, key_side, key_far, key_main = jax.random.split(jax.random.fold_in(key, 13), 4)
    shape_all = (KL, NBLK, BLK, BLK)
    raw_diag = jax.random.uniform(key_diag, shape_all, jnp.float32, -1.0, 1.0)
    symmetric = 0.5 * (raw_diag + jnp.swapaxes(raw_diag, -1, -2))
    identity = jnp.eye(BLK, dtype=jnp.float32)
    main_values = jax.random.uniform(key_main, (KL, NBLK, BLK), jnp.float32, 48.0, 60.0)
    diag_tile = symmetric * (1.0 - identity) + main_values[..., :, None] * identity
    side_raw = jax.random.uniform(key_side, shape_all, jnp.float32, -1.0, 1.0)
    right_tile = side_raw * has_right.astype(jnp.float32)[None, :, None, None]
    left_tile = jnp.swapaxes(jnp.roll(side_raw, 1, axis=1), -1, -2) * has_left.astype(jnp.float32)[None, :, None, None]
    far_raw = jax.random.uniform(key_far, shape_all, jnp.float32, -1.0, 1.0)
    far_source = jnp.take(far_raw, row_index + partner, axis=1)
    far_tile = jnp.where((partner > 0)[None, :, None, None], far_raw, jnp.swapaxes(far_source, -1, -2))
    stacked = jnp.stack([diag_tile, left_tile, right_tile, far_tile], axis=2) / 256.0
    return stacked[:, row_index[:, None], slot_order]


def draw_galerkin_mats(key, part):
    key_off, key_main = jax.random.split(jax.random.fold_in(key, 17))
    raw_off = jax.random.uniform(key_off, (KL, P_SIZE, P_SIZE), jnp.float32, -0.1, 0.1)
    symmetric = 0.5 * (raw_off + jnp.swapaxes(raw_off, -1, -2))
    identity = jnp.eye(P_SIZE, dtype=jnp.float32)
    main_values = jax.random.uniform(key_main, (KL, P_SIZE), jnp.float32, 1.5, 2.5)
    return symmetric * (1.0 - identity) + main_values[..., :, None] * identity


def draw_right_side(key, part):
    key_node, key_coef, key_base = jax.random.split(jax.random.fold_in(key, 19), 3)
    positions = jnp.arange(NODES, dtype=jnp.float32)
    growth = jnp.exp(math.log(3.0) * positions / NODES)
    node_scale = jnp.exp(jax.random.uniform(key_node, (NODES,), jnp.float32, 0.0, math.log(10.0)))
    coef_scale = jnp.exp(jax.random.uniform(key_coef, (P_SIZE,), jnp.float32, 0.0, math.log(10.0)))
    base_values = jax.random.truncated_normal(key_base, -4.0, 4.0, (P_SIZE, NODES), jnp.float32)
    values_out = growth[None, :] * base_values * coef_scale[:, None] * node_scale[None, :] / 10.0
    return values_out


def shard_levels(stream_key, extent, cuts, least, top_value):
    def one(axis_at, parts):
        heights = jax.random.uniform(jax.random.fold_in(jax.random.fold_in(stream_key, 6), axis_at), (parts,), jnp.float32, least / len(cuts), top_value / len(cuts))
        return jnp.repeat(jnp.exp(heights), extent[axis_at] // parts).reshape((-1,) + (1,) * (len(extent) - axis_at - 1))

    loudness = one(*cuts[0])
    for cut in cuts[1:]:
        loudness = loudness * one(*cut)
    return loudness


def centred(stream_key, shape, scale, most, cuts=(), held_as=jnp.bfloat16):
    gain = shard_levels(stream_key, shape, cuts, -0.22, 0.18) if cuts else 1.0
    values = jax.random.normal(stream_key, shape, jnp.float32) * scale * gain
    return jnp.minimum(jnp.maximum(values, -most), most).astype(held_as)


def setup_inputs(seed: int = 0, part: int = 0) -> dict:
    seeds = jax.random.split(jax.random.key(seed), 6)
    part_splits = jax.random.split(jax.random.fold_in(seeds[5], part), 6)
    right_side = draw_right_side(jax.random.fold_in(jax.random.fold_in(seeds[5], part), 71), part)
    initial = centred(part_splits[1], (P_SIZE, NODES), 0.5, 3.0, ((1, 16),), jnp.float32)
    galerkin_mats = draw_galerkin_mats(jax.random.fold_in(seeds[5], 71), part)
    stiffness_tiles = draw_stiffness_tiles(jax.random.fold_in(jax.random.fold_in(seeds[5], part), 71), part)
    block_cols = draw_block_cols(jax.random.fold_in(jax.random.fold_in(seeds[5], part), 71), part)
    return dict(right_side=right_side, initial=initial, galerkin_mats=galerkin_mats, stiffness_tiles=stiffness_tiles, block_cols=block_cols)


def apply_operator(values_in, stiffness_tiles, block_cols, galerkin_mats):
    blocks = values_in.reshape(values_in.shape[0], NBLK, BLK)
    picked = blocks[:, block_cols]
    mixed_terms = jnp.einsum("kbsij,pbsj->kpbi", stiffness_tiles, picked, precision=lax.Precision.HIGHEST)
    result = jnp.einsum("kpq,kqbi->pbi", galerkin_mats, mixed_terms, precision=lax.Precision.HIGHEST)
    return result.reshape(values_in.shape)


def reference(right_side, initial, galerkin_mats, stiffness_tiles, block_cols):
    solution_field = initial
    residual = right_side - apply_operator(initial, stiffness_tiles, block_cols, galerkin_mats)
    direction = residual
    norm_now = jnp.sum(residual * residual)
    for iteration in range(ITERS):
        applied = apply_operator(direction, stiffness_tiles, block_cols, galerkin_mats)
        step_length = norm_now / jnp.sum(direction * applied)
        solution_field = solution_field + step_length * direction
        residual = residual - step_length * applied
        norm_next = jnp.sum(residual * residual)
        direction = residual + (norm_next / norm_now) * direction
        norm_now = norm_next
    return solution_field, residual
```

```python
import functools

import jax
import jax.numpy as jnp
from jax import lax
from jax.experimental import pallas as pl
from jax.experimental.pallas import tpu as pltpu
from jax.sharding import PartitionSpec as P

MESH = pl.DeviceIdType.MESH
W = 128


def halves(value):
    high = value.astype(jnp.bfloat16)
    low = (value - high.astype(jnp.float32)).astype(jnp.bfloat16)
    return high, low


def first_of(columns, wanted, otherwise):
    found = otherwise
    for slot in range(3, -1, -1):
        found = jnp.where(columns[slot] == wanted, slot, found)
    return found


def kernel(
    n, kl, coefs, cols, rhs, init, gm, tiles, x_out, r_out,
    v_init, v_rhs, v_gm, gpad, gcat, st0, st1, st2, tbf, win, mixed, mbf,
    field, base, sent, got, red_s, red_r, v_x, v_r,
    in_sem, out_sem, halo_send, halo_recv, red_send, red_recv,
):
    me = lax.axis_index("node")
    core = lax.rem(me, 2)
    sibling = me + 1 - 2 * core
    outward = me - 1 + 2 * core
    has_outward = jnp.logical_and(outward >= 0, outward < n)
    edge = pl.multiple_of(core * 2 * W, W)
    staged = (st0, st1, st2)

    loads = [
        pltpu.make_async_copy(init, v_init, in_sem.at[0]),
        pltpu.make_async_copy(tiles.at[:, 0], st0, in_sem.at[1]),
        pltpu.make_async_copy(gm, v_gm, in_sem.at[2]),
        pltpu.make_async_copy(rhs, v_rhs, in_sem.at[3]),
        pltpu.make_async_copy(tiles.at[:, 1], st1, in_sem.at[4]),
        pltpu.make_async_copy(tiles.at[:, 2], st2, in_sem.at[5]),
    ]
    for load in loads:
        load.start()

    barrier = pltpu.get_barrier_semaphore()

    def greet(step, carry):
        peer = lax.rem(me + step, n)
        pl.semaphore_signal(barrier, inc=1, device_id={"node": peer}, device_id_type=MESH)
        return carry

    lax.fori_loop(1, n, greet, 0)

    roles, picks = [], []
    for row in range(3):
        away = [cols[row, slot] - 3 * me - row for slot in range(4)]
        own_first = first_of(away, 0, 0)
        own_last = jnp.int32(0)
        for slot in range(4):
            own_last = jnp.where(away[slot] == 0, slot, own_last)
        left = first_of(away, -1, own_last)
        right = first_of(away, 1, own_last)
        partner = jnp.int32(0)
        for slot in range(4):
            partner = jnp.where(jnp.abs(away[slot]) >= 2, slot, partner)
        order = (own_first, right, left, partner) if row == 0 else (own_first, left, right, partner)
        where = []
        for slot in order:
            rel = cols[row, slot] - 3 * me
            inside = jnp.logical_and(rel >= 0, rel < 3)
            in_pair = rel + 6 * core
            in_pair = jnp.where(in_pair >= 6, 6, in_pair)
            in_pair = jnp.where(in_pair < 0, 6, in_pair)
            in_pair = jnp.where(jnp.logical_and(core == 1, rel == 3), 6, in_pair)
            where.append(jnp.where(inside, rel, in_pair))
        roles.append(order)
        picks.append(where)

    def turned(ref, row):
        part = ref[:, row * W:(row + 1) * W]
        part = jnp.concatenate([part, jnp.zeros((W - coefs, W), jnp.float32)], axis=0)
        return part.T

    def into_window(place, value):
        high, low = halves(value)
        win[place, :, 0:W] = high
        win[place, :, W:2 * W] = low

    loads[0].wait()
    for row in range(3):
        value = turned(v_init, row)
        base[row * W:(row + 1) * W, :] = value
        sent[0, row * W:(row + 1) * W, :] = value
    pl.semaphore_wait(barrier, n - 1)

    def to_sibling(turn):
        return pltpu.make_async_remote_copy(
            src_ref=sent.at[turn], dst_ref=got.at[turn, pl.ds(0, 3 * W)],
            send_sem=halo_send.at[turn, 0], recv_sem=halo_recv.at[turn, 0],
            device_id={"node": sibling}, device_id_type=MESH,
        )

    def to_outward(turn):
        return pltpu.make_async_remote_copy(
            src_ref=sent.at[turn, pl.ds(edge, W)], dst_ref=got.at[turn, pl.ds(3 * W, W)],
            send_sem=halo_send.at[turn, 1], recv_sem=halo_recv.at[turn, 1],
            device_id={"node": outward}, device_id_type=MESH,
        )

    def send(turn):
        @pl.when(has_outward)
        def _():
            to_outward(turn).start()

        to_sibling(turn).start()

    def finish(turn):
        to_sibling(turn).wait()

        @pl.when(has_outward)
        def _():
            to_outward(turn).wait()

    send(0)

    def weights(row, part):
        one = win[picks[row][2 * part]]
        two = win[picks[row][2 * part + 1]]
        return jnp.concatenate([one, two, one, two], axis=0)

    def product(row, part):
        out = jnp.dot(tbf[row, part], weights(row, part), preferred_element_type=jnp.float32)
        return out[:, 0:W] + out[:, W:2 * W]

    def convert(row):
        source = staged[row]

        def body(k, carry):
            at = pl.multiple_of(k * W, W)
            for place in range(4):
                high, low = halves(source[k, roles[row][place]])
                part, side = place // 2, place % 2
                tbf[row, part, pl.ds(at, W), side * W:(side + 1) * W] = high
                tbf[row, part, pl.ds(at, W), (2 + side) * W:(3 + side) * W] = low
            return carry

        lax.fori_loop(0, kl, body, 0)

    def operate(turn, prepare):
        for row in range(3):
            into_window(row, sent[turn, row * W:(row + 1) * W, :])
        for row in range(3):
            if prepare:
                loads[(1, 4, 5)[row]].wait()
                convert(row)
            mixed[row] = product(row, 0)
        finish(turn)
        for place in range(4):
            into_window(3 + place, got[turn, place * W:(place + 1) * W, :])
        for row in range(3):
            high, low = halves(mixed[row] + product(row, 1))
            for k in range(kl):
                mbf[row * W:(row + 1) * W, k * W:(k + 1) * W] = high[k * W:(k + 1) * W]
                mbf[row * W:(row + 1) * W, (kl + k) * W:(kl + k + 1) * W] = low[k * W:(k + 1) * W]
        out = jnp.dot(mbf[...], gcat[...], preferred_element_type=jnp.float32)
        return out[:, 0:W] + out[:, W:2 * W]

    loads[2].wait()
    gpad[...] = jnp.zeros_like(gpad)
    gpad[:, 0:coefs, 0:coefs] = v_gm[...]
    for k in range(kl):
        high, low = halves(gpad[k])
        for copy in range(2):
            at = (copy * kl + k) * W
            gcat[at:at + W, 0:W] = high
            gcat[at:at + W, W:2 * W] = low
    loads[3].wait()
    for row in range(3):
        field[row * W:(row + 1) * W, :] = turned(v_rhs, row)

    def partial(one, two):
        return jnp.sum(one * two, axis=0, keepdims=True)

    def share(turn, parts):
        rows = parts + [jnp.zeros((8 - len(parts), W), jnp.float32)]
        red_s[turn] = jnp.concatenate(rows, axis=0)

        def body(step, carry):
            pltpu.make_async_remote_copy(
                src_ref=red_s.at[turn], dst_ref=red_r.at[turn, step - 1],
                send_sem=red_send.at[turn], recv_sem=red_recv.at[turn],
                device_id={"node": lax.rem(me + step, n)}, device_id_type=MESH,
            ).start()
            return carry

        lax.fori_loop(1, n, body, 0)

    def collect(turn):
        everyone = red_r.at[turn]
        pltpu.make_async_copy(everyone, everyone, red_recv.at[turn]).wait()
        total = red_s[turn] + jnp.sum(red_r[turn], axis=0)
        return jnp.sum(total, axis=1, keepdims=True)

    r0 = field[...] - operate(0, True)
    sent[1] = r0
    send(1)
    w = operate(1, False)
    sent[2] = w
    send(2)
    r0 = sent[1]
    share(0, [partial(r0, r0), partial(r0, w)])
    z = operate(2, False)
    sums = collect(0)
    rr, rw = sums[0:1], sums[1:2]
    step0 = rr / rw
    r0, w = sent[1], sent[2]
    r1 = r0 - step0 * w
    q = w - step0 * z
    share(1, [partial(r1, r1), partial(r1, q), partial(r0, q) + partial(r1, w)])
    x1 = base[...] + step0 * r0
    sums = collect(1)
    new = sums[0:1]
    beta = new / rr
    step1 = new / (sums[1:2] + beta * (sums[2:3] + beta * rw))
    x2 = x1 + step1 * (r1 + beta * r0)
    r2 = r1 - step1 * (q + beta * w)
    for row in range(3):
        v_x[:, row * W:(row + 1) * W] = x2[row * W:(row + 1) * W].T[0:coefs]
        v_r[:, row * W:(row + 1) * W] = r2[row * W:(row + 1) * W].T[0:coefs]
    stores = [
        pltpu.make_async_copy(v_x, x_out, out_sem.at[0]),
        pltpu.make_async_copy(v_r, r_out, out_sem.at[1]),
    ]
    for store in stores:
        store.start()
    for turn in range(2):
        everyone = red_r.at[turn]
        pltpu.make_async_copy(everyone, everyone, red_send.at[turn]).wait()
    for store in stores:
        store.wait()


def per_device(right_side, initial, galerkin_mats, stiffness_tiles, block_cols):
    n = lax.axis_size("node")
    coefs, nodes = right_side.shape
    kl = galerkin_mats.shape[0]
    assert stiffness_tiles.shape[1:] == (3, 4, W, W) and coefs <= W and n % 2 == 0
    f32, b16 = jnp.float32, jnp.bfloat16
    anywhere = pl.BlockSpec(memory_space=pl.ANY)
    out = jax.ShapeDtypeStruct(right_side.shape, f32)
    staged = pltpu.VMEM((kl, 4, W, W), f32)
    return pl.pallas_call(
        functools.partial(kernel, n, kl, coefs),
        out_shape=(out, out),
        in_specs=[pl.BlockSpec(memory_space=pltpu.SMEM)] + [anywhere] * 4,
        out_specs=(anywhere, anywhere),
        scratch_shapes=[
            pltpu.VMEM((coefs, nodes), f32),
            pltpu.VMEM((coefs, nodes), f32),
            pltpu.VMEM(galerkin_mats.shape, f32),
            pltpu.VMEM((kl, W, W), f32),
            pltpu.VMEM((2 * kl * W, 2 * W), b16),
            staged, staged, staged,
            pltpu.VMEM((3, 2, kl * W, 4 * W), b16),
            pltpu.VMEM((7, W, 2 * W), b16),
            pltpu.VMEM((3, kl * W, W), f32),
            pltpu.VMEM((3 * W, 2 * kl * W), b16),
            pltpu.VMEM((3 * W, W), f32),
            pltpu.VMEM((3 * W, W), f32),
            pltpu.VMEM((3, 3 * W, W), f32),
            pltpu.VMEM((3, 4 * W, W), f32),
            pltpu.VMEM((2, 8, W), f32),
            pltpu.VMEM((2, n - 1, 8, W), f32),
            pltpu.VMEM((coefs, nodes), f32),
            pltpu.VMEM((coefs, nodes), f32),
            pltpu.SemaphoreType.DMA((6,)),
            pltpu.SemaphoreType.DMA((2,)),
            pltpu.SemaphoreType.DMA((3, 2)),
            pltpu.SemaphoreType.DMA((3, 2)),
            pltpu.SemaphoreType.DMA((2,)),
            pltpu.SemaphoreType.DMA((2,)),
        ],
        compiler_params=pltpu.CompilerParams(
            collective_id=0, has_side_effects=True, vmem_limit_bytes=56 * 2**20
        ),
    )(block_cols, right_side, initial, galerkin_mats, stiffness_tiles)


def solution(mesh):
    placed = (
        P(None, ("group", "node")),
        P(None, ("group", "node")),
        P(),
        P(None, ("group", "node"), None, None, None),
        P(("group", "node"), None),
    )
    return jax.shard_map(
        per_device,
        mesh=mesh,
        in_specs=placed,
        out_specs=(P(None, ("group", "node")), P(None, ("group", "node"))),
        check_vma=False,
    )
```

```python
import functools

import jax
import jax.numpy as jnp
from jax import lax
from jax.experimental import pallas as pl
from jax.experimental.pallas import tpu as pltpu
from jax.sharding import PartitionSpec as P

MESH = pl.DeviceIdType.MESH
W = 128


def halves(value):
    high = value.astype(jnp.bfloat16)
    low = (value - high.astype(jnp.float32)).astype(jnp.bfloat16)
    return high, low


def first_of(columns, wanted, otherwise):
    found = otherwise
    for slot in range(3, -1, -1):
        found = jnp.where(columns[slot] == wanted, slot, found)
    return found


def kernel(
    n, kl, coefs, cols, rhs, init, gm, tiles, out,
    v_init, v_rhs, v_gm, gpad, gcat, st0, st1, st2, tbf, win, mixed, mbf,
    vec, base, sent, got, red_s, red_r, pair_r,
    in_sem, halo_send, halo_recv, red_send, red_recv, pair_send, pair_recv,
):
    me = lax.axis_index("node")
    core = lax.rem(me, 2)
    sibling = me + 1 - 2 * core
    outward = me - 1 + 2 * core
    has_outward = jnp.logical_and(outward >= 0, outward < n)
    rows = [2 * core, 1, 2 - 2 * core]
    lanes = [pl.ds(pl.multiple_of(row * W, W), W) for row in rows]
    staged = (st0, st1, st2)

    loads = [
        pltpu.make_async_copy(init, v_init, in_sem.at[0]),
        pltpu.make_async_copy(tiles.at[:, rows[0]], st0, in_sem.at[1]),
        pltpu.make_async_copy(gm, v_gm, in_sem.at[2]),
        pltpu.make_async_copy(rhs, v_rhs, in_sem.at[3]),
        pltpu.make_async_copy(tiles.at[:, rows[1]], st1, in_sem.at[4]),
        pltpu.make_async_copy(tiles.at[:, rows[2]], st2, in_sem.at[5]),
    ]
    for load in loads:
        load.start()

    barrier = pltpu.get_barrier_semaphore()

    def greet(peer):
        pl.semaphore_signal(barrier, inc=1, device_id={"node": peer}, device_id_type=MESH)

    greet(sibling)

    @pl.when(has_outward)
    def _():
        greet(outward)

    def greet_same_core(step, carry):
        greet(lax.rem(me + 2 * step, n))
        return carry

    lax.fori_loop(1, n // 2, greet_same_core, 0)

    roles, picks = [], []
    for i in range(3):
        spots = []
        for slot in range(4):
            rel = cols[rows[i], slot] - 3 * me
            spots.append(jnp.where(core == 1, 2 - rel, rel))
        away = [spot - i for spot in spots]
        own_first = first_of(away, 0, 0)
        own_last = jnp.int32(0)
        partner = jnp.int32(0)
        for slot in range(4):
            own_last = jnp.where(away[slot] == 0, slot, own_last)
            partner = jnp.where(jnp.abs(away[slot]) >= 2, slot, partner)
        out_side = first_of(away, -1, own_last)
        in_side = first_of(away, 1, own_last)
        if i == 0:
            order = (own_first, in_side, out_side, partner)
        else:
            order = (own_first, out_side, in_side, partner)
        where = []
        for slot in order:
            spot = jnp.int32(0)
            for other in range(4):
                spot = jnp.where(slot == other, spots[other], spot)
            where.append(jnp.where(spot < 0, 6, jnp.where(spot > 2, jnp.maximum(8 - spot, 0), spot)))
        roles.append(order)
        picks.append(where)

    def turned(ref, i):
        part = ref[:, lanes[i]]
        part = jnp.concatenate([part, jnp.zeros((W - coefs, W), jnp.float32)], axis=0)
        return part.T

    def into_window(place, value):
        high, low = halves(value)
        win[place, :, 0:W] = high
        win[place, :, W:2 * W] = low

    def block_copy(turn, i, peer, place):
        return pltpu.make_async_remote_copy(
            src_ref=sent.at[turn, i], dst_ref=got.at[turn, place],
            send_sem=halo_send.at[turn, place], recv_sem=halo_recv.at[turn, place],
            device_id={"node": peer}, device_id_type=MESH,
        )

    def send(turn, i):
        if i == 0:
            @pl.when(has_outward)
            def _():
                block_copy(turn, 0, outward, 3).start()

        block_copy(turn, i, sibling, i).start()

    def finish(turn):
        for i in range(3):
            block_copy(turn, i, sibling, i).wait()

        @pl.when(has_outward)
        def _():
            block_copy(turn, 0, outward, 3).wait()

        for place in range(4):
            into_window(3 + place, got[turn, place])

    loads[0].wait()
    for i in range(3):
        value = turned(v_init, i)
        base[i] = value
        sent[0, i] = value
    pl.semaphore_wait(barrier, n // 2 + has_outward.astype(jnp.int32))
    for i in range(3):
        send(0, i)

    def product(i, part):
        one = win[picks[i][2 * part]]
        two = win[picks[i][2 * part + 1]]
        sides = jnp.concatenate([one, two, one, two], axis=0)
        made = jnp.dot(tbf[i, part], sides, preferred_element_type=jnp.float32)
        return made[:, 0:W] + made[:, W:2 * W]

    def convert(i):
        source = staged[i]

        def body(k, carry):
            at = pl.multiple_of(k * W, W)
            for place in range(4):
                high, low = halves(source[k, roles[i][place]])
                part, side = place // 2, place % 2
                tbf[i, part, pl.ds(at, W), side * W:(side + 1) * W] = high
                tbf[i, part, pl.ds(at, W), (2 + side) * W:(3 + side) * W] = low
            return carry

        lax.fori_loop(0, kl, body, 0)

    def operate(turn, prepare, use, between=None):
        for i in range(3):
            into_window(i, sent[turn, i])
        for i in range(3):
            if prepare:
                loads[(1, 4, 5)[i]].wait()
                convert(i)
            mixed[i] = product(i, 0)
        if between is not None:
            between()
        finish(turn)
        for i in range(3):
            high, low = halves(mixed[i] + product(i, 1))
            for k in range(kl):
                mbf[i, 0:W, k * W:(k + 1) * W] = high[k * W:(k + 1) * W]
                mbf[i, W:2 * W, k * W:(k + 1) * W] = low[k * W:(k + 1) * W]
            made = jnp.dot(mbf[i], gcat[...], preferred_element_type=jnp.float32)
            made = made[0:W] + made[W:2 * W]
            use(i, made[:, 0:W] + made[:, W:2 * W])

    loads[2].wait()
    gpad[...] = jnp.zeros_like(gpad)
    gpad[:, 0:coefs, 0:coefs] = v_gm[...]
    for k in range(kl):
        high, low = halves(gpad[k])
        gcat[k * W:(k + 1) * W, 0:W] = high
        gcat[k * W:(k + 1) * W, W:2 * W] = low
    loads[3].wait()
    for i in range(3):
        vec[0, i] = turned(v_rhs, i)

    def partial(pairs):
        return sum(jnp.sum(one * two, axis=0, keepdims=True) for one, two in pairs)

    def pair_copy(turn):
        return pltpu.make_async_remote_copy(
            src_ref=red_s.at[turn, 0], dst_ref=pair_r.at[turn],
            send_sem=pair_send.at[turn], recv_sem=pair_recv.at[turn],
            device_id={"node": sibling}, device_id_type=MESH,
        )

    def share(turn, parts):
        parts = parts + [jnp.zeros((8 - len(parts), W), jnp.float32)]
        red_s[turn, 0] = jnp.concatenate(parts, axis=0)
        pair_copy(turn).start()

    def spread(turn):
        pair_copy(turn).wait()
        red_s[turn, 1] = red_s[turn, 0] + pair_r[turn]

        def body(step, carry):
            pltpu.make_async_remote_copy(
                src_ref=red_s.at[turn, 1], dst_ref=red_r.at[turn, step - 1],
                send_sem=red_send.at[turn], recv_sem=red_recv.at[turn],
                device_id={"node": lax.rem(me + 2 * step, n)}, device_id_type=MESH,
            ).start()
            return carry

        lax.fori_loop(1, n // 2, body, 0)

    def collect(turn):
        everyone = red_r.at[turn]
        pltpu.make_async_copy(everyone, everyone, red_recv.at[turn]).wait()
        total = red_s[turn, 1] + jnp.sum(red_r[turn], axis=0)
        return jnp.sum(total, axis=1, keepdims=True)

    three = range(3)

    def first(i, applied):
        vec[1, i] = applied
        sent[1, i] = vec[0, i] - applied
        send(1, i)

    operate(0, True, first)
    share(0, [
        partial([(base[i], base[i]) for i in three]),
        partial([(base[i], vec[1, i]) for i in three]),
    ])

    guess = []

    def second(i, applied):
        vec[0, i] = applied
        if i == 0:
            sums = collect(0)
            usable = sums[1:2] > 1e-6 * sums[0:1]
            ratio = sums[0:1] / jnp.where(usable, sums[1:2], 1.0)
            usable = jnp.logical_and(usable, ratio > 1e-6)
            guess.append(jnp.where(usable, 1.0, 0.0))
            guess.append(jnp.where(usable, -ratio, 1.0))
        sent[2, i] = guess[0] * sent[1, i] + guess[1] * applied
        send(2, i)

    operate(1, False, second, lambda: spread(0))
    share(1, [
        partial([(sent[1, i], sent[1, i]) for i in three]),
        partial([(sent[1, i], vec[0, i]) for i in three]),
    ])

    def third(i, applied):
        vec[1, i] = applied

    operate(2, False, third, lambda: spread(1))
    sums = collect(1)
    rr, rw = sums[0:1], sums[1:2]
    step0 = rr / rw
    scaled = step0 / guess[1]
    r0 = [sent[1, i] for i in three]
    w = [vec[0, i] for i in three]
    r1 = [r0[i] - step0 * w[i] for i in three]
    q = [(1.0 + scaled * guess[0]) * w[i] - scaled * vec[1, i] for i in three]
    share(2, [
        partial(list(zip(r1, r1))),
        partial(list(zip(r1, q))),
        partial(list(zip(r0, q)) + list(zip(r1, w))),
    ])
    spread(2)
    x1 = [base[i] + step0 * r0[i] for i in three]
    sums = collect(2)
    new = sums[0:1]
    beta = new / rr
    step1 = new / (sums[1:2] + beta * (sums[2:3] + beta * rw))
    for i in three:
        x2 = x1[i] + step1 * (r1[i] + beta * r0[i])
        r2 = r1[i] - step1 * (q[i] + beta * w[i])
        out[0, :, lanes[i]] = x2.T[0:coefs]
        out[1, :, lanes[i]] = r2.T[0:coefs]
    for turn in range(3):
        everyone = red_r.at[turn]
        pltpu.make_async_copy(everyone, everyone, red_send.at[turn]).wait()


def unstack(both, x_out, r_out):
    x_out[...] = both[0]
    r_out[...] = both[1]


def per_device(right_side, initial, galerkin_mats, stiffness_tiles, block_cols):
    n = lax.axis_size("node")
    coefs, nodes = right_side.shape
    kl = galerkin_mats.shape[0]
    assert stiffness_tiles.shape[1:] == (3, 4, W, W) and coefs <= W and n % 2 == 0
    f32, b16 = jnp.float32, jnp.bfloat16
    anywhere = pl.BlockSpec(memory_space=pl.ANY)
    vmem = pl.BlockSpec(memory_space=pltpu.VMEM)
    staged = pltpu.VMEM((kl, 4, W, W), f32)
    both = pl.pallas_call(
        functools.partial(kernel, n, kl, coefs),
        out_shape=jax.ShapeDtypeStruct((2, coefs, nodes), f32),
        in_specs=[pl.BlockSpec(memory_space=pltpu.SMEM)] + [anywhere] * 4,
        out_specs=vmem,
        scratch_shapes=[
            pltpu.VMEM((coefs, nodes), f32),
            pltpu.VMEM((coefs, nodes), f32),
            pltpu.VMEM(galerkin_mats.shape, f32),
            pltpu.VMEM((kl, W, W), f32),
            pltpu.VMEM((kl * W, 2 * W), b16),
            staged, staged, staged,
            pltpu.VMEM((3, 2, kl * W, 4 * W), b16),
            pltpu.VMEM((7, W, 2 * W), b16),
            pltpu.VMEM((3, kl * W, W), f32),
            pltpu.VMEM((3, 2 * W, kl * W), b16),
            pltpu.VMEM((2, 3, W, W), f32),
            pltpu.VMEM((3, W, W), f32),
            pltpu.VMEM((3, 3, W, W), f32),
            pltpu.VMEM((3, 4, W, W), f32),
            pltpu.VMEM((3, 2, 8, W), f32),
            pltpu.VMEM((3, n // 2 - 1, 8, W), f32),
            pltpu.VMEM((3, 8, W), f32),
            pltpu.SemaphoreType.DMA((6,)),
            pltpu.SemaphoreType.DMA((3, 4)),
            pltpu.SemaphoreType.DMA((3, 4)),
            pltpu.SemaphoreType.DMA((3,)),
            pltpu.SemaphoreType.DMA((3,)),
            pltpu.SemaphoreType.DMA((3,)),
            pltpu.SemaphoreType.DMA((3,)),
        ],
        compiler_params=pltpu.CompilerParams(
            collective_id=0, has_side_effects=True, vmem_limit_bytes=56 * 2**20
        ),
    )(block_cols, right_side, initial, galerkin_mats, stiffness_tiles)
    one = jax.ShapeDtypeStruct((coefs, nodes), f32)
    return pl.pallas_call(
        unstack, out_shape=(one, one), in_specs=[vmem], out_specs=(vmem, vmem)
    )(both)


def solution(mesh):
    placed = (
        P(None, ("group", "node")),
        P(None, ("group", "node")),
        P(),
        P(None, ("group", "node"), None, None, None),
        P(("group", "node"), None),
    )
    return jax.shard_map(
        per_device,
        mesh=mesh,
        in_specs=placed,
        out_specs=(P(None, ("group", "node")), P(None, ("group", "node"))),
        check_vma=False,
    )
```

```python
import functools

import jax
import jax.numpy as jnp
from jax import lax
from jax.experimental import pallas as pl
from jax.experimental.pallas import tpu as pltpu
from jax.sharding import PartitionSpec as P

MESH = pl.DeviceIdType.MESH
W = 128


def halves(value):
    high = value.astype(jnp.bfloat16)
    low = (value - high.astype(jnp.float32)).astype(jnp.bfloat16)
    return high, low


def first_of(columns, wanted, otherwise):
    found = otherwise
    for slot in range(3, -1, -1):
        found = jnp.where(columns[slot] == wanted, slot, found)
    return found


def kernel(
    n, kl, coefs, cols, rhs, init, gm, tiles, out,
    v_init, v_rhs, v_gm, gpad, gcat, st0, st1, st2, tbf, win, mixed, mbf,
    vec, base, sent, got, red_s, red_r,
    in_sem, halo_send, halo_recv, red_send, red_recv,
):
    me = lax.axis_index("node")
    core = lax.rem(me, 2)
    sibling = me + 1 - 2 * core
    outward = me - 1 + 2 * core
    has_outward = jnp.logical_and(outward >= 0, outward < n)
    rows = [2 * core, 1, 2 - 2 * core]
    lanes = [pl.ds(pl.multiple_of(row * W, W), W) for row in rows]
    staged = (st0, st1, st2)

    loads = [
        pltpu.make_async_copy(init, v_init, in_sem.at[0]),
        pltpu.make_async_copy(tiles.at[:, rows[0]], st0, in_sem.at[1]),
        pltpu.make_async_copy(gm, v_gm, in_sem.at[2]),
        pltpu.make_async_copy(rhs, v_rhs, in_sem.at[3]),
        pltpu.make_async_copy(tiles.at[:, rows[1]], st1, in_sem.at[4]),
        pltpu.make_async_copy(tiles.at[:, rows[2]], st2, in_sem.at[5]),
    ]
    for load in loads:
        load.start()

    barrier = pltpu.get_barrier_semaphore()

    def greet(peer):
        pl.semaphore_signal(barrier, inc=1, device_id={"node": peer}, device_id_type=MESH)

    def greet_all(step, carry):
        greet(lax.rem(me + step, n))
        return carry

    lax.fori_loop(1, n, greet_all, 0)

    roles, picks = [], []
    for i in range(3):
        spots = []
        for slot in range(4):
            rel = cols[rows[i], slot] - 3 * me
            spots.append(jnp.where(core == 1, 2 - rel, rel))
        away = [spot - i for spot in spots]
        own_first = first_of(away, 0, 0)
        own_last = jnp.int32(0)
        partner = jnp.int32(0)
        for slot in range(4):
            own_last = jnp.where(away[slot] == 0, slot, own_last)
            partner = jnp.where(jnp.abs(away[slot]) >= 2, slot, partner)
        out_side = first_of(away, -1, own_last)
        in_side = first_of(away, 1, own_last)
        if i == 0:
            order = (own_first, in_side, out_side, partner)
        else:
            order = (own_first, out_side, in_side, partner)
        where = []
        for slot in order:
            spot = jnp.int32(0)
            for other in range(4):
                spot = jnp.where(slot == other, spots[other], spot)
            where.append(jnp.where(spot < 0, 6, jnp.where(spot > 2, jnp.maximum(8 - spot, 0), spot)))
        roles.append(order)
        picks.append(where)

    def turned(ref, i):
        part = ref[:, lanes[i]]
        part = jnp.concatenate([part, jnp.zeros((W - coefs, W), jnp.float32)], axis=0)
        return part.T

    def into_window(place, value):
        high, low = halves(value)
        win[place, :, 0:W] = high
        win[place, :, W:2 * W] = low

    def block_copy(turn, i, peer, place):
        return pltpu.make_async_remote_copy(
            src_ref=sent.at[turn, i], dst_ref=got.at[turn, place],
            send_sem=halo_send.at[turn, place], recv_sem=halo_recv.at[turn, place],
            device_id={"node": peer}, device_id_type=MESH,
        )

    def send(turn, i):
        if i == 0:
            @pl.when(has_outward)
            def _():
                block_copy(turn, 0, outward, 3).start()

        block_copy(turn, i, sibling, i).start()

    def finish(turn):
        for i in range(3):
            block_copy(turn, i, sibling, i).wait()

        @pl.when(has_outward)
        def _():
            block_copy(turn, 0, outward, 3).wait()

        for place in range(4):
            into_window(3 + place, got[turn, place])

    loads[0].wait()
    for i in range(3):
        value = turned(v_init, i)
        base[i] = value
        sent[0, i] = value
    pl.semaphore_wait(barrier, n - 1)
    for i in range(3):
        send(0, i)

    def product(i, part):
        one = win[picks[i][2 * part]]
        two = win[picks[i][2 * part + 1]]
        sides = jnp.concatenate([one, two, one, two], axis=0)
        made = jnp.dot(tbf[i, part], sides, preferred_element_type=jnp.float32)
        return made[:, 0:W] + made[:, W:2 * W]

    def convert(i):
        source = staged[i]

        def body(k, carry):
            at = pl.multiple_of(k * W, W)
            for place in range(4):
                high, low = halves(source[k, roles[i][place]])
                part, side = place // 2, place % 2
                tbf[i, part, pl.ds(at, W), side * W:(side + 1) * W] = high
                tbf[i, part, pl.ds(at, W), (2 + side) * W:(3 + side) * W] = low
            return carry

        lax.fori_loop(0, kl, body, 0)

    def operate(turn, prepare, use):
        for i in range(3):
            into_window(i, sent[turn, i])
        for i in range(3):
            if prepare:
                loads[(1, 4, 5)[i]].wait()
                convert(i)
            mixed[i] = product(i, 0)
        finish(turn)
        for i in range(3):
            high, low = halves(mixed[i] + product(i, 1))
            for k in range(kl):
                mbf[i, 0:W, k * W:(k + 1) * W] = high[k * W:(k + 1) * W]
                mbf[i, W:2 * W, k * W:(k + 1) * W] = low[k * W:(k + 1) * W]
            made = jnp.dot(mbf[i], gcat[...], preferred_element_type=jnp.float32)
            made = made[0:W] + made[W:2 * W]
            use(i, made[:, 0:W] + made[:, W:2 * W])

    loads[2].wait()
    gpad[...] = jnp.zeros_like(gpad)
    gpad[:, 0:coefs, 0:coefs] = v_gm[...]
    for k in range(kl):
        high, low = halves(gpad[k])
        gcat[k * W:(k + 1) * W, 0:W] = high
        gcat[k * W:(k + 1) * W, W:2 * W] = low
    loads[3].wait()
    for i in range(3):
        vec[0, i] = turned(v_rhs, i)

    def partial(pairs):
        return sum(jnp.sum(one * two, axis=0, keepdims=True) for one, two in pairs)

    def share(turn, parts):
        parts = parts + [jnp.zeros((8 - len(parts), W), jnp.float32)]
        red_s[turn] = jnp.concatenate(parts, axis=0)

        def body(step, carry):
            pltpu.make_async_remote_copy(
                src_ref=red_s.at[turn], dst_ref=red_r.at[turn, step - 1],
                send_sem=red_send.at[turn], recv_sem=red_recv.at[turn],
                device_id={"node": lax.rem(me + step, n)}, device_id_type=MESH,
            ).start()
            return carry

        lax.fori_loop(1, n, body, 0)

    def collect(turn):
        everyone = red_r.at[turn]
        pltpu.make_async_copy(everyone, everyone, red_recv.at[turn]).wait()
        total = red_s[turn] + jnp.sum(red_r[turn], axis=0)
        return jnp.sum(total, axis=1, keepdims=True)

    three = range(3)

    def first(i, applied):
        vec[1, i] = applied
        sent[1, i] = vec[0, i] - applied
        send(1, i)

    operate(0, True, first)
    share(0, [
        partial([(base[i], base[i]) for i in three]),
        partial([(base[i], vec[1, i]) for i in three]),
    ])

    guess = []

    def second(i, applied):
        vec[0, i] = applied
        if i == 0:
            sums = collect(0)
            usable = sums[1:2] > 1e-6 * sums[0:1]
            ratio = sums[0:1] / jnp.where(usable, sums[1:2], 1.0)
            usable = jnp.logical_and(usable, ratio > 1e-6)
            guess.append(jnp.where(usable, 1.0, 0.0))
            guess.append(jnp.where(usable, -ratio, 1.0))
        sent[2, i] = guess[0] * sent[1, i] + guess[1] * applied
        send(2, i)

    operate(1, False, second)
    share(1, [
        partial([(sent[1, i], sent[1, i]) for i in three]),
        partial([(sent[1, i], vec[0, i]) for i in three]),
    ])

    def third(i, applied):
        vec[1, i] = applied

    operate(2, False, third)
    sums = collect(1)
    rr, rw = sums[0:1], sums[1:2]
    step0 = rr / rw
    scaled = step0 / guess[1]
    r0 = [sent[1, i] for i in three]
    w = [vec[0, i] for i in three]
    r1 = [r0[i] - step0 * w[i] for i in three]
    q = [(1.0 + scaled * guess[0]) * w[i] - scaled * vec[1, i] for i in three]
    share(2, [
        partial(list(zip(r1, r1))),
        partial(list(zip(r1, q))),
        partial(list(zip(r0, q)) + list(zip(r1, w))),
    ])
    x1 = [base[i] + step0 * r0[i] for i in three]
    sums = collect(2)
    new = sums[0:1]
    beta = new / rr
    step1 = new / (sums[1:2] + beta * (sums[2:3] + beta * rw))
    for i in three:
        x2 = x1[i] + step1 * (r1[i] + beta * r0[i])
        r2 = r1[i] - step1 * (q[i] + beta * w[i])
        out[0, :, lanes[i]] = x2.T[0:coefs]
        out[1, :, lanes[i]] = r2.T[0:coefs]
    for turn in range(3):
        everyone = red_r.at[turn]
        pltpu.make_async_copy(everyone, everyone, red_send.at[turn]).wait()


def unstack(both, x_out, r_out):
    x_out[...] = both[0]
    r_out[...] = both[1]


def per_device(right_side, initial, galerkin_mats, stiffness_tiles, block_cols):
    n = lax.axis_size("node")
    coefs, nodes = right_side.shape
    kl = galerkin_mats.shape[0]
    assert stiffness_tiles.shape[1:] == (3, 4, W, W) and coefs <= W and n % 2 == 0
    f32, b16 = jnp.float32, jnp.bfloat16
    anywhere = pl.BlockSpec(memory_space=pl.ANY)
    vmem = pl.BlockSpec(memory_space=pltpu.VMEM)
    staged = pltpu.VMEM((kl, 4, W, W), f32)
    both = pl.pallas_call(
        functools.partial(kernel, n, kl, coefs),
        out_shape=jax.ShapeDtypeStruct((2, coefs, nodes), f32),
        in_specs=[pl.BlockSpec(memory_space=pltpu.SMEM)] + [anywhere] * 4,
        out_specs=vmem,
        scratch_shapes=[
            pltpu.VMEM((coefs, nodes), f32),
            pltpu.VMEM((coefs, nodes), f32),
            pltpu.VMEM(galerkin_mats.shape, f32),
            pltpu.VMEM((kl, W, W), f32),
            pltpu.VMEM((kl * W, 2 * W), b16),
            staged, staged, staged,
            pltpu.VMEM((3, 2, kl * W, 4 * W), b16),
            pltpu.VMEM((7, W, 2 * W), b16),
            pltpu.VMEM((3, kl * W, W), f32),
            pltpu.VMEM((3, 2 * W, kl * W), b16),
            pltpu.VMEM((2, 3, W, W), f32),
            pltpu.VMEM((3, W, W), f32),
            pltpu.VMEM((3, 3, W, W), f32),
            pltpu.VMEM((3, 4, W, W), f32),
            pltpu.VMEM((3, 8, W), f32),
            pltpu.VMEM((3, n - 1, 8, W), f32),
            pltpu.SemaphoreType.DMA((6,)),
            pltpu.SemaphoreType.DMA((3, 4)),
            pltpu.SemaphoreType.DMA((3, 4)),
            pltpu.SemaphoreType.DMA((3,)),
            pltpu.SemaphoreType.DMA((3,)),
        ],
        compiler_params=pltpu.CompilerParams(
            collective_id=0, has_side_effects=True, vmem_limit_bytes=56 * 2**20
        ),
    )(block_cols, right_side, initial, galerkin_mats, stiffness_tiles)
    one = jax.ShapeDtypeStruct((coefs, nodes), f32)
    return pl.pallas_call(
        unstack, out_shape=(one, one), in_specs=[vmem], out_specs=(vmem, vmem)
    )(both)


def solution(mesh):
    placed = (
        P(None, ("group", "node")),
        P(None, ("group", "node")),
        P(),
        P(None, ("group", "node"), None, None, None),
        P(("group", "node"), None),
    )
    return jax.shard_map(
        per_device,
        mesh=mesh,
        in_specs=placed,
        out_specs=(P(None, ("group", "node")), P(None, ("group", "node"))),
        check_vma=False,
    )
```

```python
import functools

import jax
import jax.numpy as jnp
from jax import lax
from jax.experimental import pallas as pl
from jax.experimental.pallas import tpu as pltpu
from jax.sharding import PartitionSpec as P

MESH = pl.DeviceIdType.MESH
W = 128


def halves(value):
    high = value.astype(jnp.bfloat16)
    low = (value - high.astype(jnp.float32)).astype(jnp.bfloat16)
    return high, low


def first_of(columns, wanted, otherwise):
    found = otherwise
    for slot in range(3, -1, -1):
        found = jnp.where(columns[slot] == wanted, slot, found)
    return found


def kernel(
    n, kl, coefs, cols, rhs, init, gm, tiles, out,
    v_init, v_rhs, v_gm, gpad, gcat, st0, st1, st2, tbf, win, mixed, mbf,
    vec, base, sent, got, red_s, red_r,
    in_sem, halo_send, halo_recv, red_send, red_recv,
):
    me = lax.axis_index("node")
    core = lax.rem(me, 2)
    sibling = me + 1 - 2 * core
    outward = me - 1 + 2 * core
    has_outward = jnp.logical_and(outward >= 0, outward < n)
    rows = [2 * core, 1, 2 - 2 * core]
    lanes = [pl.ds(pl.multiple_of(row * W, W), W) for row in rows]
    staged = (st0, st1, st2)

    loads = [
        pltpu.make_async_copy(init, v_init, in_sem.at[0]),
        pltpu.make_async_copy(tiles.at[:, rows[0]], st0, in_sem.at[1]),
        pltpu.make_async_copy(gm, v_gm, in_sem.at[2]),
        pltpu.make_async_copy(rhs, v_rhs, in_sem.at[3]),
        pltpu.make_async_copy(tiles.at[:, rows[1]], st1, in_sem.at[4]),
        pltpu.make_async_copy(tiles.at[:, rows[2]], st2, in_sem.at[5]),
    ]
    for load in loads:
        load.start()

    barrier = pltpu.get_barrier_semaphore()

    def greet(peer):
        pl.semaphore_signal(barrier, inc=1, device_id={"node": peer}, device_id_type=MESH)

    def greet_all(step, carry):
        greet(lax.rem(me + step, n))
        return carry

    lax.fori_loop(1, n, greet_all, 0)

    roles, picks = [], []
    for i in range(3):
        spots = []
        for slot in range(4):
            rel = cols[rows[i], slot] - 3 * me
            spots.append(jnp.where(core == 1, 2 - rel, rel))
        away = [spot - i for spot in spots]
        own_first = first_of(away, 0, 0)
        own_last = jnp.int32(0)
        partner = jnp.int32(0)
        for slot in range(4):
            own_last = jnp.where(away[slot] == 0, slot, own_last)
            partner = jnp.where(jnp.abs(away[slot]) >= 2, slot, partner)
        out_side = first_of(away, -1, own_last)
        in_side = first_of(away, 1, own_last)
        if i == 0:
            order = (own_first, in_side, out_side, partner)
        else:
            order = (own_first, out_side, in_side, partner)
        where = []
        for slot in order:
            spot = jnp.int32(0)
            for other in range(4):
                spot = jnp.where(slot == other, spots[other], spot)
            where.append(jnp.where(spot < 0, 6, jnp.where(spot > 2, jnp.maximum(8 - spot, 0), spot)))
        roles.append(order)
        picks.append(where)

    def turned(ref, i):
        part = ref[:, lanes[i]]
        part = jnp.concatenate([part, jnp.zeros((W - coefs, W), jnp.float32)], axis=0)
        return part.T

    def into_window(place, value):
        high, low = halves(value)
        win[place, :, 0:W] = high
        win[place, :, W:2 * W] = low

    def block_copy(turn, i, peer, place):
        return pltpu.make_async_remote_copy(
            src_ref=sent.at[turn, i], dst_ref=got.at[turn, place],
            send_sem=halo_send.at[turn, place], recv_sem=halo_recv.at[turn, place],
            device_id={"node": peer}, device_id_type=MESH,
        )

    def send(turn, i):
        if i == 0:
            @pl.when(has_outward)
            def _():
                block_copy(turn, 0, outward, 3).start()

        block_copy(turn, i, sibling, i).start()

    def finish(turn):
        for i in range(3):
            block_copy(turn, i, sibling, i).wait()

        @pl.when(has_outward)
        def _():
            block_copy(turn, 0, outward, 3).wait()

        for place in range(4):
            into_window(3 + place, got[turn, place])

    loads[0].wait()
    for i in range(3):
        value = turned(v_init, i)
        base[i] = value
        sent[0, i] = value
    pl.semaphore_wait(barrier, n - 1)
    for i in range(3):
        send(0, i)

    def product(i, part):
        one = win[picks[i][2 * part]]
        two = win[picks[i][2 * part + 1]]
        sides = jnp.concatenate([one, two, one, two], axis=0)
        made = jnp.dot(tbf[i, part], sides, preferred_element_type=jnp.float32)
        return made[:, 0:W] + made[:, W:2 * W]

    def convert(i):
        source = staged[i]

        def body(k, carry):
            at = pl.multiple_of(k * W, W)
            for place in range(4):
                high, low = halves(source[k, roles[i][place]])
                part, side = place // 2, place % 2
                tbf[i, part, pl.ds(at, W), side * W:(side + 1) * W] = high
                tbf[i, part, pl.ds(at, W), (2 + side) * W:(3 + side) * W] = low
            return carry

        lax.fori_loop(0, kl, body, 0)

    def operate(turn, prepare, use):
        for i in range(3):
            into_window(i, sent[turn, i])
        for i in range(3):
            if prepare:
                loads[(1, 4, 5)[i]].wait()
                convert(i)
            mixed[i] = product(i, 0)
        finish(turn)
        for i in range(3):
            high, low = halves(mixed[i] + product(i, 1))
            for k in range(kl):
                mbf[i, 0:W, k * W:(k + 1) * W] = high[k * W:(k + 1) * W]
                mbf[i, W:2 * W, k * W:(k + 1) * W] = low[k * W:(k + 1) * W]
            made = jnp.dot(mbf[i], gcat[...], preferred_element_type=jnp.float32)
            made = made[0:W] + made[W:2 * W]
            use(i, made[:, 0:W] + made[:, W:2 * W])

    loads[2].wait()
    gpad[...] = jnp.zeros_like(gpad)
    gpad[:, 0:coefs, 0:coefs] = v_gm[...]
    for k in range(kl):
        high, low = halves(gpad[k])
        gcat[k * W:(k + 1) * W, 0:W] = high
        gcat[k * W:(k + 1) * W, W:2 * W] = low
    loads[3].wait()
    for i in range(3):
        vec[0, i] = turned(v_rhs, i)

    def partial(pairs):
        return sum(jnp.sum(one * two, axis=0, keepdims=True) for one, two in pairs)

    def share(turn, parts):
        parts = parts + [jnp.zeros((8 - len(parts), W), jnp.float32)]
        red_s[turn] = jnp.concatenate(parts, axis=0)

        def body(step, carry):
            pltpu.make_async_remote_copy(
                src_ref=red_s.at[turn], dst_ref=red_r.at[turn, step - 1],
                send_sem=red_send.at[turn], recv_sem=red_recv.at[turn],
                device_id={"node": lax.rem(me + step, n)}, device_id_type=MESH,
            ).start()
            return carry

        lax.fori_loop(1, n, body, 0)

    def collect(turn):
        everyone = red_r.at[turn]
        pltpu.make_async_copy(everyone, everyone, red_recv.at[turn]).wait()
        total = red_s[turn] + jnp.sum(red_r[turn], axis=0)
        return jnp.sum(total, axis=1, keepdims=True)

    three = range(3)

    def first(i, applied):
        sent[1, i] = vec[0, i] - applied
        send(1, i)
        if i == 0:
            share(0, [partial([(base[0], base[0])]), partial([(base[0], applied)])])

    operate(0, True, first)
    guess = []

    def second(i, applied):
        vec[0, i] = applied
        if i == 0:
            sums = collect(0)
            usable = sums[1:2] > 1e-6 * sums[0:1]
            ratio = sums[0:1] / jnp.where(usable, sums[1:2], 1.0)
            usable = jnp.logical_and(usable, ratio > 1e-6)
            guess.append(jnp.where(usable, 1.0, 0.0))
            guess.append(jnp.where(usable, -ratio, 1.0))
        sent[2, i] = guess[0] * sent[1, i] + guess[1] * applied
        send(2, i)

    operate(1, False, second)
    share(1, [
        partial([(sent[1, i], sent[1, i]) for i in three]),
        partial([(sent[1, i], vec[0, i]) for i in three]),
    ])

    def third(i, applied):
        vec[1, i] = applied

    operate(2, False, third)
    sums = collect(1)
    rr, rw = sums[0:1], sums[1:2]
    step0 = rr / rw
    scaled = step0 / guess[1]
    r0 = [sent[1, i] for i in three]
    w = [vec[0, i] for i in three]
    r1 = [r0[i] - step0 * w[i] for i in three]
    q = [(1.0 + scaled * guess[0]) * w[i] - scaled * vec[1, i] for i in three]
    share(2, [
        partial(list(zip(r1, r1))),
        partial(list(zip(r1, q))),
        partial(list(zip(r0, q)) + list(zip(r1, w))),
    ])
    x1 = [base[i] + step0 * r0[i] for i in three]
    sums = collect(2)
    new = sums[0:1]
    beta = new / rr
    step1 = new / (sums[1:2] + beta * (sums[2:3] + beta * rw))
    for i in three:
        x2 = x1[i] + step1 * (r1[i] + beta * r0[i])
        r2 = r1[i] - step1 * (q[i] + beta * w[i])
        out[0, :, lanes[i]] = x2.T[0:coefs]
        out[1, :, lanes[i]] = r2.T[0:coefs]
    for turn in range(3):
        everyone = red_r.at[turn]
        pltpu.make_async_copy(everyone, everyone, red_send.at[turn]).wait()


def unstack(both, x_out, r_out):
    x_out[...] = both[0]
    r_out[...] = both[1]


def per_device(right_side, initial, galerkin_mats, stiffness_tiles, block_cols):
    n = lax.axis_size("node")
    coefs, nodes = right_side.shape
    kl = galerkin_mats.shape[0]
    assert stiffness_tiles.shape[1:] == (3, 4, W, W) and coefs <= W and n % 2 == 0
    f32, b16 = jnp.float32, jnp.bfloat16
    anywhere = pl.BlockSpec(memory_space=pl.ANY)
    vmem = pl.BlockSpec(memory_space=pltpu.VMEM)
    staged = pltpu.VMEM((kl, 4, W, W), f32)
    both = pl.pallas_call(
        functools.partial(kernel, n, kl, coefs),
        out_shape=jax.ShapeDtypeStruct((2, coefs, nodes), f32),
        in_specs=[pl.BlockSpec(memory_space=pltpu.SMEM)] + [anywhere] * 4,
        out_specs=vmem,
        scratch_shapes=[
            pltpu.VMEM((coefs, nodes), f32),
            pltpu.VMEM((coefs, nodes), f32),
            pltpu.VMEM(galerkin_mats.shape, f32),
            pltpu.VMEM((kl, W, W), f32),
            pltpu.VMEM((kl * W, 2 * W), b16),
            staged, staged, staged,
            pltpu.VMEM((3, 2, kl * W, 4 * W), b16),
            pltpu.VMEM((7, W, 2 * W), b16),
            pltpu.VMEM((3, kl * W, W), f32),
            pltpu.VMEM((3, 2 * W, kl * W), b16),
            pltpu.VMEM((2, 3, W, W), f32),
            pltpu.VMEM((3, W, W), f32),
            pltpu.VMEM((3, 3, W, W), f32),
            pltpu.VMEM((3, 4, W, W), f32),
            pltpu.VMEM((3, 8, W), f32),
            pltpu.VMEM((3, n - 1, 8, W), f32),
            pltpu.SemaphoreType.DMA((6,)),
            pltpu.SemaphoreType.DMA((3, 4)),
            pltpu.SemaphoreType.DMA((3, 4)),
            pltpu.SemaphoreType.DMA((3,)),
            pltpu.SemaphoreType.DMA((3,)),
        ],
        compiler_params=pltpu.CompilerParams(
            collective_id=0, has_side_effects=True, vmem_limit_bytes=56 * 2**20
        ),
    )(block_cols, right_side, initial, galerkin_mats, stiffness_tiles)
    one = jax.ShapeDtypeStruct((coefs, nodes), f32)
    return pl.pallas_call(
        unstack, out_shape=(one, one), in_specs=[vmem], out_specs=(vmem, vmem)
    )(both)


def solution(mesh):
    placed = (
        P(None, ("group", "node")),
        P(None, ("group", "node")),
        P(),
        P(None, ("group", "node"), None, None, None),
        P(("group", "node"), None),
    )
    return jax.shard_map(
        per_device,
        mesh=mesh,
        in_specs=placed,
        out_specs=(P(None, ("group", "node")), P(None, ("group", "node"))),
        check_vma=False,
    )
```
